256 devices in a mesh: fsdp: 64 (over z, y, x_lo), dp: 4 (over x_hi, core).
Axes of the slice: x: 4 (x_hi: 2, x_lo: 2; x = x_hi * 2 + x_lo), y: 4, z: 8, core: 2. Of those that a mesh axis runs over, the one named last changes fastest.
Arguments:
- grads: bfloat16 [4, 1024, 64, 1024], P('dp', 'fsdp'), may hold values from -4 to 4
- weights: float32 [1024, 64, 1024], P('fsdp', None, 'dp'), may hold values from -6 to 6
- moment_first: float32 [64, 1024, 1024], P('fsdp', None, 'dp'), may hold values from -3 to 3
- moment_second: float32 [64, 1024, 1024], P('fsdp', None, 'dp'), may hold values from 0.05 to 5
- left_basis: bfloat16 [64, 1024, 1024], P('fsdp'), may hold values from -0.1875 to 0.1875
- right_basis: bfloat16 [64, 1024, 1024], P('fsdp', 'dp'), may hold values from -0.1875 to 0.1875
Outputs:
- new_weights: float32 [1024, 64, 1024], P('fsdp', None, 'dp')
- new_first: float32 [64, 1024, 1024], P('fsdp', None, 'dp')
- new_second: float32 [64, 1024, 1024], P('fsdp', None, 'dp')
The draws below stay inside these ranges and needn't reach their ends.
All inputs are finite; a program needn't handle non-finite values.
Results may differ from the reference program's by a relative error of at most 0.008.
Values may be sent and summed in bfloat16 or wider, within the bound.
No kernel may reach another device: no remote copies, remote signals or barrier semaphores. Data moves between devices by JAX's collectives and lax.ppermute only.
A program may use at most 64 MiB of HBM per device.

```python
import math
import jax
import jax.numpy as jnp
from jax import lax

BS = 1024
NB = 64
N_DP = 4


def steps_of(own_key, shape, pieces, low, largest):
    factor_of, own = 1.0, jax.random.fold_in(own_key, 6)
    for position, parts in pieces:
        draws = jnp.exp(jax.random.uniform(jax.random.fold_in(own, position), (parts,), jnp.float32, low / len(pieces), largest / len(pieces)))
        factor_of = factor_of * jnp.repeat(draws, shape[position] // parts).reshape([-1 if axis == position else 1 for axis in range(len(shape))])
    return factor_of


def noise(rng, dims, deviation, bound, shards=(), kind=jnp.bfloat16):
    result = deviation * jax.random.normal(rng, dims, jnp.float32)
    if shards:
        result = result * steps_of(rng, dims, shards, -0.22, 0.18)
    return jnp.clip(result, -bound, bound).astype(kind)


def setup_inputs(seed: int = 0) -> dict:
    key_of = jax.random.split(jax.random.key(seed), 7)
    grads = noise(key_of[0], (N_DP, BS, NB, BS), 0.5, 4.0, ((0, 4), (1, 64)))
    weights = noise(key_of[1], (BS, NB, BS), 1.0, 6.0, ((0, 64), (2, 4)), jnp.float32)
    moment_first = noise(key_of[2], (NB, BS, BS), 0.3, 3.0, ((0, 64), (2, 4)), jnp.float32)
    moment_second = jnp.clip(jnp.exp(math.log(5.0) - 4.6051702 * jax.random.uniform(key_of[3], (NB, BS, BS), jnp.float32) ** steps_of(key_of[3], (NB, BS, BS), ((0, 64), (2, 4)), -0.2, 0.2)), 0.05, 5.0)
    left_basis = noise(key_of[4], (NB, BS, BS), BS ** -0.5, 0.1875, ((0, 64),))
    right_basis = noise(key_of[5], (NB, BS, BS), BS ** -0.5, 0.1875, ((0, 64), (1, 4)))
    return dict(grads=grads, weights=weights, moment_first=moment_first, moment_second=moment_second, left_basis=left_basis, right_basis=right_basis)


def reference(grads, weights, moment_first, moment_second, left_basis, right_basis):
    grad_sum = lax.optimization_barrier(jnp.sum(grads.astype(jnp.float32), axis=0)).astype(jnp.bfloat16)
    grad_blocks = jnp.transpose(grad_sum, (1, 0, 2))
    weight_blocks = jnp.transpose(weights, (1, 0, 2))
    quarter = BS // N_DP
    bias_first = 1.0 - 0.9 ** 10
    bias_second = 1.0 - 0.95 ** 10

    def one_block(items):
        grad_block, weight_block, first_old, second_old, left_block, right_block = items
        rotated_left = jnp.dot(left_block.T, grad_block, preferred_element_type=jnp.float32).astype(jnp.bfloat16)
        rotated = jnp.zeros((BS, BS), jnp.float32)
        for group in range(N_DP):
            term = jnp.dot(rotated_left[:, group * quarter:(group + 1) * quarter], right_block[group * quarter:(group + 1) * quarter, :], preferred_element_type=jnp.float32).astype(jnp.bfloat16)
            term = lax.optimization_barrier(term)
            rotated = rotated + term.astype(jnp.float32)
        first_new = 0.9 * first_old + 0.1 * rotated
        second_new = 0.95 * second_old + 0.05 * rotated * rotated
        direction = (first_new / bias_first / (jnp.sqrt(second_new / bias_second) + 1e-08)).astype(jnp.bfloat16)
        turned = jnp.dot(direction, right_block.T, preferred_element_type=jnp.float32).astype(jnp.bfloat16)
        update = jnp.dot(left_block, turned, preferred_element_type=jnp.float32)
        return (weight_block - 0.5 * update, first_new, second_new)
    new_blocks, new_first, new_second = lax.map(one_block, (grad_blocks, weight_blocks, moment_first, moment_second, left_basis, right_basis))
    new_weights = jnp.transpose(new_blocks, (1, 0, 2))
    return (new_weights, new_first, new_second)
```

```python
import jax
import jax.numpy as jnp
from jax import lax
from jax.sharding import Mesh, PartitionSpec as P

FSDP = ("z", "y", "x_lo")
DP = ("x_hi", "core")
SWAP = [(0, 1), (1, 0)]
F32 = jnp.float32
BF16 = jnp.bfloat16
Q = 256


def dot_f32(a, b, dims):
    return lax.dot_general(a, b, (dims, ((), ())), preferred_element_type=F32)


def local(grads, weights, moment_first, moment_second, left_basis, right_basis):
    core, x_hi = lax.axis_index("core"), lax.axis_index("x_hi")
    left = left_basis[0]
    right_own = right_basis[0]
    rows = grads.shape[1]
    blocks = grads.shape[2]

    low, high = right_own[:, : 2 * Q], right_own[:, 2 * Q :]
    right_half = jnp.where(x_hi == 0, low, high)
    right_far = lax.ppermute(jnp.where(x_hi == 0, high, low), "x_hi", SWAP)

    def part_of(half, which):
        return jnp.where(which == 0, half[:, :Q], half[:, Q:])

    right_cross = lax.ppermute(
        jnp.stack([part_of(right_half, 1 - core), part_of(right_far, 1 - core)]), "core", SWAP
    )

    turned_rows = jnp.transpose(grads[0], (1, 0, 2))

    def groups_of(which):
        return jnp.stack(
            [part_of(turned_rows[:, :, : 2 * Q].reshape(blocks * rows, 2 * Q), which).reshape(blocks, rows, Q),
             part_of(turned_rows[:, :, 2 * Q :].reshape(blocks * rows, 2 * Q), which).reshape(blocks, rows, Q)],
            axis=1,
        )

    arrived = lax.ppermute(groups_of(1 - core), "core", SWAP)
    chip_sum = (groups_of(core).astype(F32) + arrived.astype(F32)).astype(BF16)

    pieces = lax.all_to_all(
        chip_sum.reshape(2 * blocks, rows, Q), FSDP + ("x_hi",), split_axis=0, concat_axis=0, tiled=True
    ).reshape(blocks, 2, rows, Q)
    grad_block = (
        (pieces[:, 0].astype(F32) + pieces[:, 1].astype(F32)).astype(BF16).reshape(blocks * rows, Q)
    )

    rl_own = dot_f32(left, grad_block, ((0,), (0,))).astype(BF16)
    rl_far = lax.ppermute(rl_own, "x_hi", SWAP)
    rl_near = lax.ppermute(rl_own, "core", SWAP)
    rl_cross = lax.ppermute(rl_far, "core", SWAP)
    plain = ((1,), (0,))
    rotated = (
        dot_f32(rl_own, part_of(right_half, core), plain)
        + dot_f32(rl_near, right_cross[0], plain)
        + dot_f32(rl_far, part_of(right_far, core), plain)
        + dot_f32(rl_cross, right_cross[1], plain)
    )

    bias_first = 1.0 - 0.9**10
    bias_second = 1.0 - 0.95**10
    first_new = 0.9 * moment_first[0] + 0.1 * rotated
    second_new = 0.95 * moment_second[0] + 0.05 * rotated * rotated
    direction = (first_new / bias_first / (jnp.sqrt(second_new / bias_second) + 1e-08)).astype(BF16)

    near = lax.ppermute(direction, "core", SWAP)
    both = jnp.concatenate(
        [jnp.where(core == 0, direction, near), jnp.where(core == 0, near, direction)], axis=1
    )
    shares = []
    for group in range(2):
        right_rows = jnp.where(x_hi == group, right_half, right_far)
        turned = dot_f32(both, right_rows, ((1,), (1,))).astype(BF16)
        shares.append(dot_f32(left, turned, plain).astype(BF16).reshape(blocks, rows, Q))
    returned = lax.all_to_all(
        jnp.stack(shares, axis=1).reshape(2 * blocks, rows, Q),
        FSDP + ("x_hi",),
        split_axis=0,
        concat_axis=0,
        tiled=True,
    ).reshape(blocks, 2, rows, Q)
    update = jnp.transpose(returned[:, 0].astype(F32) + returned[:, 1].astype(F32), (1, 0, 2))
    new_weights = weights - 0.5 * update
    return (new_weights, first_new[None], second_new[None])


def solution(mesh):
    fine = Mesh(mesh.devices.reshape(8, 4, 2, 2, 2), FSDP + DP)
    placed = (
        P(DP, FSDP, None, None),
        P(FSDP, None, DP),
        P(FSDP, None, DP),
        P(FSDP, None, DP),
        P(FSDP, None, None),
        P(FSDP, DP, None),
    )
    return jax.shard_map(
        local,
        mesh=fine,
        in_specs=placed,
        out_specs=(P(FSDP, None, DP), P(FSDP, None, DP), P(FSDP, None, DP)),
        check_vma=False,
    )
```

```python
import jax
import jax.numpy as jnp
from jax import lax
from jax.experimental import pallas as pl
from jax.experimental.pallas import tpu as pltpu
from jax.sharding import Mesh, PartitionSpec as P

FSDP = ("z", "y", "x_lo")
DP = ("x_hi", "core")
SWAP = [(0, 1), (1, 0)]
F32 = jnp.float32
BF16 = jnp.bfloat16
BS = 1024
NB = 64
ROWS = 16
Q = 256
PLAIN = ((1,), (0,))
PARAMS = pltpu.CompilerParams(vmem_limit_bytes=16 << 20)


def dot_f32(a, b, dims=PLAIN):
    return lax.dot_general(a, b, (dims, ((), ())), preferred_element_type=F32)


def cost(flops, moved):
    return pl.CostEstimate(flops=flops, bytes_accessed=moved, transcendentals=0)


def swap_matrix():
    to = lax.broadcasted_iota(jnp.int32, (Q, Q), 0)
    come = lax.broadcasted_iota(jnp.int32, (Q, Q), 1)
    hit = (to // ROWS == come % ROWS) & (to % ROWS == come // ROWS)
    return jnp.where(hit, 1.0, 0.0).astype(BF16)


def pick_kernel(core_ref, grads_ref, out_ref):
    out_ref[0] = grads_ref[...]


def pick(core, grads):
    return pl.pallas_call(
        pick_kernel,
        grid_spec=pltpu.PrefetchScalarGridSpec(
            num_scalar_prefetch=1,
            grid=(2,),
            in_specs=[pl.BlockSpec((ROWS, NB, Q), lambda g, core: (0, 0, 2 * g + 1 - core[0]))],
            out_specs=pl.BlockSpec((1, ROWS, NB, Q), lambda g, core: (g, 0, 0, 0)),
        ),
        out_shape=jax.ShapeDtypeStruct((2, ROWS, NB, Q), BF16),
        compiler_params=PARAMS,
        cost_estimate=cost(0, 4 << 20),
        name="pick",
    )(core, grads)


def pack_kernel(core_ref, grads_ref, arrived_ref, out_ref):
    swap = swap_matrix()
    for part in range(NB // ROWS):
        here = pl.ds(part * ROWS, ROWS)
        total = dot_f32(swap, grads_ref[:, here, :].reshape(Q, Q))
        total += dot_f32(swap, arrived_ref[0, :, here, :].reshape(Q, Q))
        out_ref[here, 0] = total.astype(BF16).reshape(ROWS, ROWS, Q)


def pack(core, grads, arrived):
    return pl.pallas_call(
        pack_kernel,
        grid_spec=pltpu.PrefetchScalarGridSpec(
            num_scalar_prefetch=1,
            grid=(2,),
            in_specs=[
                pl.BlockSpec((ROWS, NB, Q), lambda g, core: (0, 0, 2 * g + core[0])),
                pl.BlockSpec((1, ROWS, NB, Q), lambda g, core: (g, 0, 0, 0)),
            ],
            out_specs=pl.BlockSpec((NB, 1, ROWS, Q), lambda g, core: (0, g, 0, 0)),
        ),
        out_shape=jax.ShapeDtypeStruct((NB, 2, ROWS, Q), BF16),
        compiler_params=PARAMS,
        cost_estimate=cost(4 * BS * Q * Q, 3 << 20),
        name="pack",
    )(core, grads, arrived)


def adam_kernel(own, near, far, cross, r_own, r_near, r_far, r_cross, m1, m2, first, second, direction):
    rotated = dot_f32(own[...], r_own[...]) + dot_f32(near[...], r_near[...])
    rotated += dot_f32(far[...], r_far[...]) + dot_f32(cross[...], r_cross[...])
    new1 = 0.9 * m1[0] + 0.1 * rotated
    new2 = 0.95 * m2[0] + 0.05 * rotated * rotated
    first[0] = new1
    second[0] = new2
    bias_first = 1.0 - 0.9**10
    bias_second = 1.0 - 0.95**10
    direction[...] = (new1 / bias_first / (jnp.sqrt(new2 / bias_second) + 1e-08)).astype(BF16)


def adam(terms, rights, moment_first, moment_second):
    tile = 256
    rows = pl.BlockSpec((tile, Q), lambda i: (i, 0))
    whole = pl.BlockSpec((Q, Q), lambda i: (0, 0))
    moment = pl.BlockSpec((1, tile, Q), lambda i: (0, i, 0))
    return pl.pallas_call(
        adam_kernel,
        grid=(BS // tile,),
        in_specs=[rows] * 4 + [whole] * 4 + [moment] * 2,
        out_specs=[moment, moment, rows],
        out_shape=[
            jax.ShapeDtypeStruct((1, BS, Q), F32),
            jax.ShapeDtypeStruct((1, BS, Q), F32),
            jax.ShapeDtypeStruct((BS, Q), BF16),
        ],
        compiler_params=PARAMS,
        cost_estimate=cost(8 * BS * Q * Q, 7 << 20),
        name="adam",
    )(*terms, *rights, moment_first, moment_second)


def update_kernel(own, near, r_own, r_near, left, out, turned):
    @pl.when(pl.program_id(0) == 0)
    def _():
        both = ((1,), (1,))
        total = dot_f32(own[...], r_own[...], both) + dot_f32(near[...], r_near[...], both)
        turned[...] = total.astype(BF16)

    share = dot_f32(left[...], turned[...]).astype(BF16)
    for group in range(2):
        out[:, group] = share[:, group * Q : (group + 1) * Q].reshape(out.shape[0], ROWS, Q)


def update(own, near, r_own, r_near, left):
    tile = 256
    whole = pl.BlockSpec((BS, Q), lambda i: (0, 0))
    right = pl.BlockSpec((2 * Q, Q), lambda i: (0, 0))
    return pl.pallas_call(
        update_kernel,
        grid=(BS // tile,),
        in_specs=[whole, whole, right, right, pl.BlockSpec((tile, BS), lambda i: (i, 0))],
        out_specs=pl.BlockSpec((tile // ROWS, 2, ROWS, Q), lambda i: (i, 0, 0, 0)),
        out_shape=jax.ShapeDtypeStruct((NB, 2, ROWS, Q), BF16),
        scratch_shapes=[pltpu.VMEM((BS, 2 * Q), BF16)],
        compiler_params=PARAMS,
        cost_estimate=cost(2 * BS * BS * 2 * Q + 8 * BS * Q * Q, 5 << 20),
        name="update",
    )(own, near, r_own, r_near, left)


def apply_kernel(pieces, weights, out):
    swap = swap_matrix()
    total = dot_f32(swap, pieces[:, 0].reshape(Q, Q)) + dot_f32(swap, pieces[:, 1].reshape(Q, Q))
    out[...] = weights[...] - 0.5 * total.reshape(ROWS, ROWS, Q)


def apply(pieces, weights):
    held = pl.BlockSpec((ROWS, ROWS, Q), lambda i: (0, i, 0))
    return pl.pallas_call(
        apply_kernel,
        grid=(NB // ROWS,),
        in_specs=[pl.BlockSpec((ROWS, 2, ROWS, Q), lambda i: (i, 0, 0, 0)), held],
        out_specs=held,
        out_shape=jax.ShapeDtypeStruct((ROWS, NB, Q), F32),
        compiler_params=PARAMS,
        cost_estimate=cost(4 * BS * Q * Q, 3 << 20),
        name="apply",
    )(pieces, weights)


def exchange(pieces):
    return lax.all_to_all(
        pieces.reshape(2 * NB, ROWS, Q), FSDP + ("x_hi",), split_axis=0, concat_axis=0, tiled=True
    ).reshape(NB, 2, ROWS, Q)


def local(grads, weights, moment_first, moment_second, left_basis, right_basis):
    core, x_hi = lax.axis_index("core"), lax.axis_index("x_hi")
    core_ref = core.astype(jnp.int32).reshape(1)
    left = left_basis[0]

    arrived = lax.ppermute(pick(core_ref, grads[0]), "core", SWAP)
    pieces = exchange(pack(core_ref, grads[0], arrived))

    low, high = right_basis[0, :, : 2 * Q], right_basis[0, :, 2 * Q :]
    right_half = jnp.where(x_hi == 0, low, high)
    right_far = lax.ppermute(jnp.where(x_hi == 0, high, low), "x_hi", SWAP)

    def part_of(half, which):
        return jnp.where(which == 0, half[:, :Q], half[:, Q:])

    r_own, r_far = part_of(right_half, core), part_of(right_far, core)
    n_own, n_far = part_of(right_half, 1 - core), part_of(right_far, 1 - core)
    r_near = lax.ppermute(n_own, "core", SWAP)
    r_cross = lax.ppermute(n_far, "core", SWAP)

    def by_chip(own, far):
        return jnp.where(x_hi == 0, jnp.concatenate([own, far]), jnp.concatenate([far, own]))

    rows_own, rows_near = by_chip(r_own, r_far), by_chip(n_own, n_far)

    grad_block = (pieces[:, 0].astype(F32) + pieces[:, 1].astype(F32)).astype(BF16).reshape(BS, Q)
    rl_own = dot_f32(left, grad_block, ((0,), (0,))).astype(BF16)
    rl_far = lax.ppermute(rl_own, "x_hi", SWAP)
    rl_near = lax.ppermute(rl_own, "core", SWAP)
    rl_cross = lax.ppermute(rl_far, "core", SWAP)
    first_new, second_new, direction = adam(
        (rl_own, rl_near, rl_far, rl_cross), (r_own, r_near, r_far, r_cross), moment_first, moment_second
    )
    near = lax.ppermute(direction, "core", SWAP)
    returned = exchange(update(direction, near, rows_own, rows_near, left))
    return (apply(returned, weights), first_new, second_new)


def solution(mesh):
    fine = Mesh(mesh.devices.reshape(8, 4, 2, 2, 2), FSDP + DP)
    placed = (
        P(DP, FSDP, None, None),
        P(FSDP, None, DP),
        P(FSDP, None, DP),
        P(FSDP, None, DP),
        P(FSDP, None, None),
        P(FSDP, DP, None),
    )
    return jax.shard_map(
        local,
        mesh=fine,
        in_specs=placed,
        out_specs=(P(FSDP, None, DP), P(FSDP, None, DP), P(FSDP, None, DP)),
        check_vma=False,
    )
```

```python
import jax
import jax.numpy as jnp
from jax import lax
from jax.experimental import pallas as pl
from jax.experimental.pallas import tpu as pltpu
from jax.sharding import Mesh, PartitionSpec as P

FSDP = ("z", "y", "x_lo")
DP = ("x_hi", "core")
SWAP = [(0, 1), (1, 0)]
F32 = jnp.float32
BF16 = jnp.bfloat16
BS = 1024
NB = 64
ROWS = 16
Q = 256
H = 128
PLAIN = ((1,), (0,))
WIDE = pltpu.CompilerParams(vmem_limit_bytes=60 << 20)
PARAMS = pltpu.CompilerParams(vmem_limit_bytes=16 << 20)


def dot_f32(a, b, dims=PLAIN):
    return lax.dot_general(a, b, (dims, ((), ())), preferred_element_type=F32)


def cost(flops, moved):
    return pl.CostEstimate(flops=flops, bytes_accessed=moved, transcendentals=0)


def swap_matrix():
    to = lax.broadcasted_iota(jnp.int32, (Q, Q), 0)
    come = lax.broadcasted_iota(jnp.int32, (Q, Q), 1)
    hit = (to // ROWS == come % ROWS) & (to % ROWS == come // ROWS)
    return jnp.where(hit, 1.0, 0.0).astype(BF16)


def pick_kernel(at_ref, grads_ref, out_ref):
    out_ref[0] = grads_ref[...]


def pick(at, grads):
    return pl.pallas_call(
        pick_kernel,
        grid_spec=pltpu.PrefetchScalarGridSpec(
            num_scalar_prefetch=1,
            grid=(2,),
            in_specs=[pl.BlockSpec((ROWS, NB, H), lambda g, at: (0, 0, 4 * g + at[0]))],
            out_specs=pl.BlockSpec((1, ROWS, NB, H), lambda g, at: (g, 0, 0, 0)),
        ),
        out_shape=jax.ShapeDtypeStruct((2, ROWS, NB, H), BF16),
        compiler_params=WIDE,
        cost_estimate=cost(0, 2 << 20),
        name="pick",
    )(at, grads)


def pair_sum(grads_ref, arrived_ref, store):
    swap = swap_matrix()
    for part in range(NB // ROWS):
        here = pl.ds(part * ROWS, ROWS)
        total = dot_f32(swap, grads_ref[:, here, :].reshape(Q, H))
        total += dot_f32(swap, arrived_ref[0, :, here, :].reshape(Q, H))
        store(here, total.astype(BF16).reshape(ROWS, ROWS, H))


def pack_both_kernel(at_ref, grads_ref, arrived_ref, out_ref):
    def store(here, value):
        out_ref[here, 0] = value

    pair_sum(grads_ref, arrived_ref, store)


def pack_both(at, grads, arrived):
    return pl.pallas_call(
        pack_both_kernel,
        grid_spec=pltpu.PrefetchScalarGridSpec(
            num_scalar_prefetch=1,
            grid=(2,),
            in_specs=[
                pl.BlockSpec((ROWS, NB, H), lambda g, at: (0, 0, 4 * g + at[0])),
                pl.BlockSpec((1, ROWS, NB, H), lambda g, at: (g, 0, 0, 0)),
            ],
            out_specs=pl.BlockSpec((NB, 1, ROWS, H), lambda g, at: (0, g, 0, 0)),
        ),
        out_shape=jax.ShapeDtypeStruct((NB, 2, ROWS, H), BF16),
        compiler_params=WIDE,
        cost_estimate=cost(4 * BS * Q * Q, 2 << 20),
        name="pack_both",
    )(at, grads, arrived)


def pack_one_kernel(at_ref, grads_ref, arrived_ref, out_ref):
    def store(here, value):
        out_ref[here] = value

    pair_sum(grads_ref, arrived_ref, store)


def pack_one(at, grads, arrived):
    return pl.pallas_call(
        pack_one_kernel,
        grid_spec=pltpu.PrefetchScalarGridSpec(
            num_scalar_prefetch=1,
            grid=(1,),
            in_specs=[
                pl.BlockSpec((ROWS, NB, H), lambda g, at: (0, 0, at[0])),
                pl.BlockSpec((1, ROWS, NB, H), lambda g, at: (at[1], 0, 0, 0)),
            ],
            out_specs=pl.BlockSpec((NB, ROWS, H), lambda g, at: (0, 0, 0)),
        ),
        out_shape=jax.ShapeDtypeStruct((NB, ROWS, H), BF16),
        compiler_params=PARAMS,
        cost_estimate=cost(2 * BS * Q * Q, 1 << 20),
        name="pack_one",
    )(at, grads, arrived)


def double_kernel(here, there, out):
    total = (here[...].astype(F32) + there[...].astype(F32)).astype(BF16)
    out[:, 0] = total
    out[:, 1] = total


def double(here, there):
    part = NB // 2
    held = pl.BlockSpec((part, ROWS, H), lambda i: (i, 0, 0))
    return pl.pallas_call(
        double_kernel,
        grid=(2,),
        in_specs=[held, held],
        out_specs=pl.BlockSpec((part, 2, ROWS, H), lambda i: (i, 0, 0, 0)),
        out_shape=jax.ShapeDtypeStruct((NB, 2, ROWS, H), BF16),
        compiler_params=PARAMS,
        cost_estimate=cost(1 << 18, 1 << 20),
        name="double",
    )(here, there)


def total_kernel(pieces, after, more, out):
    total = pieces[:, 0].astype(F32) + pieces[:, 1].astype(F32)
    out[...] = total.astype(BF16).reshape(BS, H)


def total(pieces, after, more):
    return pl.pallas_call(
        total_kernel,
        grid=(1,),
        in_specs=[
            pl.BlockSpec((NB, 2, ROWS, H), lambda i: (0, 0, 0, 0)),
            pl.BlockSpec(memory_space=pl.ANY),
            pl.BlockSpec(memory_space=pl.ANY),
        ],
        out_specs=pl.BlockSpec((BS, H), lambda i: (0, 0)),
        out_shape=jax.ShapeDtypeStruct((BS, H), BF16),
        compiler_params=PARAMS,
        cost_estimate=cost(1 << 18, 1 << 20),
        name="total",
    )(pieces, after, more)


def join_kernel(pieces, after, out):
    for group in range(2):
        out[:, group * H : (group + 1) * H] = pieces[:, group].reshape(BS, H)


def join(pieces, after):
    return pl.pallas_call(
        join_kernel,
        grid=(1,),
        in_specs=[
            pl.BlockSpec((NB, 2, ROWS, H), lambda i: (0, 0, 0, 0)),
            pl.BlockSpec(memory_space=pl.ANY),
        ],
        out_specs=pl.BlockSpec((BS, Q), lambda i: (0, 0)),
        out_shape=jax.ShapeDtypeStruct((BS, Q), BF16),
        compiler_params=PARAMS,
        cost_estimate=cost(0, 1 << 20),
        name="join",
    )(pieces, after)


def adam_kernel(chip, own, far, near, cross, mine, other, r_mine, r_other, m1, m2, first, second, direction):
    def side(left_a, left_b, b, right):
        a = jnp.concatenate([left_a[...], left_b[...]], axis=1)
        right_a = right[:, :H].reshape(Q, Q)
        right_b = jnp.concatenate([right[chip[0], H:], right[1 - chip[0], H:]], axis=0)
        return dot_f32(a, right_a) + dot_f32(b[...], right_b)

    rotated = side(own, far, mine, r_mine) + side(near, cross, other, r_other)
    new1 = 0.9 * m1[0] + 0.1 * rotated
    new2 = 0.95 * m2[0] + 0.05 * rotated * rotated
    first[0] = new1
    second[0] = new2
    bias_first = 1.0 - 0.9**10
    bias_second = 1.0 - 0.95**10
    direction[...] = (new1 / bias_first / (jnp.sqrt(new2 / bias_second) + 1e-08)).astype(BF16)


def adam(chip, halves, wholes, rights, moment_first, moment_second):
    tile = 256
    half = pl.BlockSpec((tile, H), lambda i, chip: (i, 0))
    rows = pl.BlockSpec((tile, Q), lambda i, chip: (i, 0))
    right = pl.BlockSpec((2, Q, Q), lambda i, chip: (0, 0, 0))
    moment = pl.BlockSpec((1, tile, Q), lambda i, chip: (0, i, 0))
    return pl.pallas_call(
        adam_kernel,
        grid_spec=pltpu.PrefetchScalarGridSpec(
            num_scalar_prefetch=1,
            grid=(BS // tile,),
            in_specs=[half] * 4 + [rows] * 2 + [right] * 2 + [moment] * 2,
            out_specs=[moment, moment, rows],
        ),
        out_shape=[
            jax.ShapeDtypeStruct((1, BS, Q), F32),
            jax.ShapeDtypeStruct((1, BS, Q), F32),
            jax.ShapeDtypeStruct((BS, Q), BF16),
        ],
        compiler_params=PARAMS,
        cost_estimate=cost(8 * BS * Q * Q, 7 << 20),
        name="adam",
    )(chip, *halves, *wholes, *rights, moment_first, moment_second)


def update_kernel(chip, own, near, r_own, r_near, left, out, turned):
    @pl.when(pl.program_id(0) == 0)
    def _():
        both = ((1,), (1,))
        for group in range(2):
            at = chip[0] if group == 0 else 1 - chip[0]
            total = dot_f32(own[...], r_own[at], both) + dot_f32(near[...], r_near[at], both)
            turned[:, group * Q : (group + 1) * Q] = total.astype(BF16)

    share = dot_f32(left[...], turned[...]).astype(BF16)
    for group in range(2):
        out[:, group] = share[:, group * Q : (group + 1) * Q].reshape(out.shape[0], ROWS, Q)


def update(chip, own, near, r_own, r_near, left):
    tile = 256
    whole = pl.BlockSpec((BS, Q), lambda i, chip: (0, 0))
    right = pl.BlockSpec((2, Q, Q), lambda i, chip: (0, 0, 0))
    return pl.pallas_call(
        update_kernel,
        grid_spec=pltpu.PrefetchScalarGridSpec(
            num_scalar_prefetch=1,
            grid=(BS // tile,),
            in_specs=[whole, whole, right, right, pl.BlockSpec((tile, BS), lambda i, chip: (i, 0))],
            out_specs=pl.BlockSpec((tile // ROWS, 2, ROWS, Q), lambda i, chip: (i, 0, 0, 0)),
            scratch_shapes=[pltpu.VMEM((BS, 2 * Q), BF16)],
        ),
        out_shape=jax.ShapeDtypeStruct((NB, 2, ROWS, Q), BF16),
        compiler_params=PARAMS,
        cost_estimate=cost(2 * BS * BS * 2 * Q + 8 * BS * Q * Q, 5 << 20),
        name="update",
    )(chip, own, near, r_own, r_near, left)


def apply_kernel(pieces, weights, out):
    swap = swap_matrix()
    total = dot_f32(swap, pieces[:, 0].reshape(Q, Q)) + dot_f32(swap, pieces[:, 1].reshape(Q, Q))
    out[...] = weights[...] - 0.5 * total.reshape(ROWS, ROWS, Q)


def apply(pieces, weights):
    held = pl.BlockSpec((ROWS, ROWS, Q), lambda i: (0, i, 0))
    return pl.pallas_call(
        apply_kernel,
        grid=(NB // ROWS,),
        in_specs=[pl.BlockSpec((ROWS, 2, ROWS, Q), lambda i: (i, 0, 0, 0)), held],
        out_specs=held,
        out_shape=jax.ShapeDtypeStruct((ROWS, NB, Q), F32),
        compiler_params=PARAMS,
        cost_estimate=cost(4 * BS * Q * Q, 3 << 20),
        name="apply",
    )(pieces, weights)


def exchange(pieces):
    width = pieces.shape[-1]
    return lax.all_to_all(
        pieces.reshape(2 * NB, ROWS, width), FSDP + ("x_hi",), split_axis=0, concat_axis=0, tiled=True
    ).reshape(NB, 2, ROWS, width)


def local(grads, weights, moment_first, moment_second, left_basis, right_basis):
    core = lax.axis_index("core").astype(jnp.int32)
    x_hi = lax.axis_index("x_hi").astype(jnp.int32)
    slab = grads[0]
    left = left_basis[0]

    mine, other = 2 * core, 2 * (1 - core)
    sent_a = lax.ppermute(pick(other.reshape(1), slab), "core", SWAP)
    sent_b = lax.ppermute(pick((other + 1).reshape(1), slab), "core", SWAP)

    pieces_a = exchange(pack_both(mine.reshape(1), slab, sent_a))

    def group_b(group):
        return pack_one(jnp.stack([4 * group + mine + 1, group]), slab, sent_b)

    far_b = lax.ppermute(group_b(1 - x_hi), "x_hi", SWAP)
    both_b = double(group_b(x_hi), far_b)
    pieces_b = exchange(both_b)

    low, high = right_basis[0, :, : 2 * Q], right_basis[0, :, 2 * Q :]
    right_half = jnp.where(x_hi == 0, low, high)
    right_far = lax.ppermute(jnp.where(x_hi == 0, high, low), "x_hi", SWAP)
    right_rows = jnp.stack([right_half, right_far])
    r_mine = jnp.where(core == 0, right_rows[:, :, :Q], right_rows[:, :, Q:])
    r_near = jnp.where(core == 0, right_rows[:, :, Q:], right_rows[:, :, :Q])
    r_other = lax.ppermute(r_near, "core", SWAP)

    rl_a = dot_f32(left, total(pieces_a, both_b, r_other), ((0,), (0,))).astype(BF16)
    far_a = lax.ppermute(rl_a, "x_hi", SWAP)
    near_a = lax.ppermute(rl_a, "core", SWAP)
    cross_a = lax.ppermute(far_a, "core", SWAP)
    rl_b = dot_f32(left, join(pieces_b, far_a), ((0,), (0,))).astype(BF16)
    chip = x_hi.reshape(1)
    first_new, second_new, direction = adam(
        chip,
        (rl_a, far_a, near_a, cross_a),
        (rl_b, lax.ppermute(rl_b, "core", SWAP)),
        (r_mine, r_other),
        moment_first,
        moment_second,
    )
    near = lax.ppermute(direction, "core", SWAP)
    share = update(chip, direction, near, r_mine, r_near, left)
    return (apply(exchange(share), weights), first_new, second_new)


def solution(mesh):
    fine = Mesh(mesh.devices.reshape(8, 4, 2, 2, 2), FSDP + DP)
    placed = (
        P(DP, FSDP, None, None),
        P(FSDP, None, DP),
        P(FSDP, None, DP),
        P(FSDP, None, DP),
        P(FSDP, None, None),
        P(FSDP, DP, None),
    )
    return jax.shard_map(
        local,
        mesh=fine,
        in_specs=placed,
        out_specs=(P(FSDP, None, DP), P(FSDP, None, DP), P(FSDP, None, DP)),
        check_vma=False,
    )
```

```python
import jax
import jax.numpy as jnp
from jax import lax
from jax.experimental import pallas as pl
from jax.experimental.pallas import tpu as pltpu
from jax.sharding import Mesh, PartitionSpec as P

FSDP = ("z", "y", "x_lo")
DP = ("x_hi", "core")
SWAP = [(0, 1), (1, 0)]
F32 = jnp.float32
BF16 = jnp.bfloat16
BS = 1024
NB = 64
ROWS = 16
Q = 256
PARTS = 2
PLAIN = ((1,), (0,))
PARAMS = pltpu.CompilerParams(vmem_limit_bytes=16 << 20)


def dot_f32(a, b, dims=PLAIN):
    return lax.dot_general(a, b, (dims, ((), ())), preferred_element_type=F32)


def cost(flops, moved):
    return pl.CostEstimate(flops=flops, bytes_accessed=moved, transcendentals=0)


def swap_matrix():
    to = lax.broadcasted_iota(jnp.int32, (Q, Q), 0)
    come = lax.broadcasted_iota(jnp.int32, (Q, Q), 1)
    hit = (to // ROWS == come % ROWS) & (to % ROWS == come // ROWS)
    return jnp.where(hit, 1.0, 0.0).astype(BF16)


def pick_kernel(core_ref, grads_ref, out_ref):
    out_ref[0] = grads_ref[...]


def pick(core, grads):
    return pl.pallas_call(
        pick_kernel,
        grid_spec=pltpu.PrefetchScalarGridSpec(
            num_scalar_prefetch=1,
            grid=(2,),
            in_specs=[pl.BlockSpec((ROWS, NB, Q), lambda g, core: (0, 0, 2 * g + 1 - core[0]))],
            out_specs=pl.BlockSpec((1, ROWS, NB, Q), lambda g, core: (g, 0, 0, 0)),
        ),
        out_shape=jax.ShapeDtypeStruct((2, ROWS, NB, Q), BF16),
        compiler_params=PARAMS,
        cost_estimate=cost(0, 4 << 20),
        name="pick",
    )(core, grads)


def pack_kernel(core_ref, grads_ref, arrived_ref, out_ref):
    swap = swap_matrix()
    for part in range(NB // ROWS):
        here = pl.ds(part * ROWS, ROWS)
        total = dot_f32(swap, grads_ref[:, here, :].reshape(Q, Q))
        total += dot_f32(swap, arrived_ref[0, :, here, :].reshape(Q, Q))
        out_ref[here] = total.astype(BF16).reshape(ROWS, ROWS, Q)


def pack(core, grads, arrived):
    return pl.pallas_call(
        pack_kernel,
        grid_spec=pltpu.PrefetchScalarGridSpec(
            num_scalar_prefetch=1,
            grid=(2,),
            in_specs=[
                pl.BlockSpec((ROWS, NB, Q), lambda g, core: (0, 0, 2 * g + core[0])),
                pl.BlockSpec((1, ROWS, NB, Q), lambda g, core: (g, 0, 0, 0)),
            ],
            out_specs=pl.BlockSpec((NB, ROWS, Q), lambda g, core: (0, 0, g)),
        ),
        out_shape=jax.ShapeDtypeStruct((NB, ROWS, 2 * Q), BF16),
        compiler_params=PARAMS,
        cost_estimate=cost(4 * BS * Q * Q, 3 << 20),
        name="pack",
    )(core, grads, arrived)


def term_kernel(at, left_own, left_far, own_send, far_send, own_keep, far_keep, send, keep):
    send[0] = (dot_f32(left_own[...], own_send[...]) + dot_f32(left_far[...], far_send[...])).astype(BF16)
    keep[0] = dot_f32(left_own[...], own_keep[...]) + dot_f32(left_far[...], far_keep[...])


def term(at, left, right_own, right_far):
    size = BS // PARTS

    def right(other):
        return pl.BlockSpec((Q, Q), lambda g, at: (0, 2 * g + (1 - at[1] if other else at[1])))

    held = pl.BlockSpec((1, size, Q), lambda g, at: (g, 0, 0))
    return pl.pallas_call(
        term_kernel,
        grid_spec=pltpu.PrefetchScalarGridSpec(
            num_scalar_prefetch=1,
            grid=(2,),
            in_specs=[
                pl.BlockSpec((size, Q), lambda g, at: (0, at[0])),
                pl.BlockSpec((size, Q), lambda g, at: (0, 1 - at[0])),
                right(True),
                right(True),
                right(False),
                right(False),
            ],
            out_specs=[held, held],
        ),
        out_shape=[jax.ShapeDtypeStruct((2, size, Q), BF16), jax.ShapeDtypeStruct((2, size, Q), F32)],
        compiler_params=PARAMS,
        cost_estimate=cost(16 * size * Q * Q, 4 << 20),
        name="term",
    )(at, left, left, right_own, right_far, right_own, right_far)


def chip_kernel(at, far_keep, far_arrived, own_keep, own_arrived, send, keep):
    send[...] = (far_keep[0] + far_arrived[0].astype(F32)).astype(BF16)
    keep[...] = own_keep[0] + own_arrived[0].astype(F32)


def chip_sum(at, keep, arrived):
    size = BS // PARTS
    far = pl.BlockSpec((1, size, Q), lambda i, at: (1 - at[0], 0, 0))
    own = pl.BlockSpec((1, size, Q), lambda i, at: (at[0], 0, 0))
    held = pl.BlockSpec((size, Q), lambda i, at: (0, 0))
    return pl.pallas_call(
        chip_kernel,
        grid_spec=pltpu.PrefetchScalarGridSpec(
            num_scalar_prefetch=1, grid=(1,), in_specs=[far, far, own, own], out_specs=[held, held]
        ),
        out_shape=[jax.ShapeDtypeStruct((size, Q), BF16), jax.ShapeDtypeStruct((size, Q), F32)],
        compiler_params=PARAMS,
        cost_estimate=cost(4 * size * Q, 1 << 20),
        name="chip_sum",
    )(at, keep, arrived, keep, arrived)


def adam_kernel(own, far, m1, m2, *rest):
    first, second, direction = rest[-3:]
    rotated = own[...] + far[...].astype(F32)
    new1 = 0.9 * m1[0] + 0.1 * rotated
    new2 = 0.95 * m2[0] + 0.05 * rotated * rotated
    first[0] = new1
    second[0] = new2
    bias_first = 1.0 - 0.9**10
    bias_second = 1.0 - 0.95**10
    direction[...] = (new1 / bias_first / (jnp.sqrt(new2 / bias_second) + 1e-08)).astype(BF16)


def adam(part, own, far, moments, done):
    tile = 256
    steps = BS // PARTS // tile
    rows = pl.BlockSpec((tile, Q), lambda i: (i, 0))
    moment = pl.BlockSpec((1, tile, Q), lambda i: (0, steps * part + i, 0))
    return pl.pallas_call(
        adam_kernel,
        grid=(steps,),
        in_specs=[rows] * 2 + [moment] * 2 + [pl.BlockSpec(memory_space=pl.ANY)] * len(done),
        out_specs=[moment, moment, rows],
        out_shape=[
            jax.ShapeDtypeStruct((1, BS, Q), F32),
            jax.ShapeDtypeStruct((1, BS, Q), F32),
            jax.ShapeDtypeStruct((BS // PARTS, Q), BF16),
        ],
        input_output_aliases={4 + n: n for n in range(len(done))},
        compiler_params=PARAMS,
        cost_estimate=cost(1 << 18, 1 << 18),
        name="adam",
    )(own, far, *moments, *done)


def far_kernel(at, own0, own1, near0, near1, own_own, own_near, far_own, far_near, left, out, turned, far):
    @pl.when(pl.program_id(0) == 0)
    def _():
        both = ((1,), (1,))
        for part, (own, near) in enumerate(((own0, near0), (own1, near1))):
            rows = slice(part * BS // PARTS, (part + 1) * BS // PARTS)
            for r_own, r_near, to in ((own_own, own_near, turned), (far_own, far_near, far)):
                total = dot_f32(own[...], r_own[...], both) + dot_f32(near[...], r_near[...], both)
                to[rows] = total.astype(BF16)

    out[...] = dot_f32(left[...], far[...]).astype(BF16).reshape(out.shape)


def far_share(at, own, near, right_own, right_far, left):
    tile = 256
    half = pl.BlockSpec((BS // PARTS, Q), lambda i, at: (0, 0))
    r_own = pl.BlockSpec((Q, Q), lambda i, at: (0, 2 * at[0] + at[1]))
    r_near = pl.BlockSpec((Q, Q), lambda i, at: (0, 2 * at[0] + 1 - at[1]))
    return pl.pallas_call(
        far_kernel,
        grid_spec=pltpu.PrefetchScalarGridSpec(
            num_scalar_prefetch=1,
            grid=(BS // tile,),
            in_specs=[half] * 4 + [r_own, r_near] * 2 + [pl.BlockSpec((tile, BS), lambda i, at: (i, 0))],
            out_specs=[
                pl.BlockSpec((tile // ROWS, ROWS, Q), lambda i, at: (i, 0, 0)),
                pl.BlockSpec((BS, Q), lambda i, at: (0, 0)),
            ],
            scratch_shapes=[pltpu.VMEM((BS, Q), BF16)],
        ),
        out_shape=[
            jax.ShapeDtypeStruct((NB, ROWS, Q), BF16),
            jax.ShapeDtypeStruct((BS, Q), BF16),
        ],
        compiler_params=PARAMS,
        cost_estimate=cost(2 * BS * BS * Q + 8 * BS * Q * Q, 5 << 20),
        name="far_share",
    )(at, *own, *near, right_own, right_own, right_far, right_far, left)


def own_kernel(left, turned, out):
    out[...] = dot_f32(left[...], turned[...]).reshape(out.shape)


def own_share(left, turned):
    tile = 256
    return pl.pallas_call(
        own_kernel,
        grid=(BS // tile,),
        in_specs=[pl.BlockSpec((tile, BS), lambda i: (i, 0)), pl.BlockSpec((BS, Q), lambda i: (0, 0))],
        out_specs=pl.BlockSpec((tile // ROWS, ROWS, Q), lambda i: (i, 0, 0)),
        out_shape=jax.ShapeDtypeStruct((NB, ROWS, Q), F32),
        compiler_params=PARAMS,
        cost_estimate=cost(2 * BS * BS * Q, 4 << 20),
        name="own_share",
    )(left, turned)


def add_kernel(here, there, out):
    out[...] = (here[...] + there[...].astype(F32)).astype(BF16)


def add(here, there):
    held = pl.BlockSpec((NB, ROWS, Q), lambda i: (0, 0, 0))
    return pl.pallas_call(
        add_kernel,
        grid=(1,),
        in_specs=[held, held],
        out_specs=held,
        out_shape=jax.ShapeDtypeStruct((NB, ROWS, Q), BF16),
        compiler_params=PARAMS,
        cost_estimate=cost(1 << 18, 2 << 20),
        name="add",
    )(here, there)


def apply_kernel(pieces, weights, out):
    total = dot_f32(swap_matrix(), pieces[...].reshape(Q, Q))
    out[...] = weights[...] - 0.5 * total.reshape(ROWS, ROWS, Q)


def apply(pieces, weights):
    held = pl.BlockSpec((ROWS, ROWS, Q), lambda i: (0, i, 0))
    return pl.pallas_call(
        apply_kernel,
        grid=(NB // ROWS,),
        in_specs=[pl.BlockSpec((ROWS, ROWS, Q), lambda i: (i, 0, 0)), held],
        out_specs=held,
        out_shape=jax.ShapeDtypeStruct((ROWS, NB, Q), F32),
        compiler_params=PARAMS,
        cost_estimate=cost(2 * BS * Q * Q, 3 << 20),
        name="apply",
    )(pieces, weights)


def exchange(pieces, axes):
    return lax.all_to_all(pieces, axes, split_axis=0, concat_axis=0, tiled=True)


def local(grads, weights, moment_first, moment_second, left_basis, right_basis):
    core = lax.axis_index("core").astype(jnp.int32)
    x_hi = lax.axis_index("x_hi").astype(jnp.int32)
    core_ref = core.reshape(1)
    left = left_basis[0]

    at = jnp.stack([x_hi, core])

    arrived = lax.ppermute(pick(core_ref, grads[0]), "core", SWAP)
    pieces = exchange(pack(core_ref, grads[0], arrived), FSDP)
    right_own = right_basis[0]
    right_far = lax.ppermute(right_own, "x_hi", SWAP)
    pieces, right_far = lax.optimization_barrier((pieces, right_far))

    half = BS // PARTS
    grad_block = pieces.reshape(BS, 2 * Q)
    parts = range(PARTS)
    sent, kept = [], []
    for part in parts:
        rotated_left = dot_f32(left[:, part * half : (part + 1) * half], grad_block, ((0,), (0,))).astype(BF16)
        send, keep = term(at, rotated_left, right_own, right_far)
        sent.append(lax.ppermute(send, "core", SWAP))
        kept.append(keep)
    sums = [chip_sum(at, kept[part], sent[part]) for part in parts]
    far = [lax.ppermute(send, "x_hi", SWAP) for send, _ in sums]
    done, own, near = (), [], []
    for part in parts:
        if part:
            far[part], own[-1] = lax.optimization_barrier((far[part], own[-1]))
        *done, direction = adam(part, sums[part][1], far[part], (moment_first, moment_second), done)
        own.append(direction)
        near.append(lax.ppermute(direction, "core", SWAP))

    far, turned = far_share(at, own, near, right_own, right_far, left)
    there = lax.ppermute(far, "x_hi", SWAP)
    returned = exchange(add(own_share(left, turned), there), FSDP)
    return (apply(returned, weights), *done)


def solution(mesh):
    fine = Mesh(mesh.devices.reshape(8, 4, 2, 2, 2), FSDP + DP)
    placed = (
        P(DP, FSDP, None, None),
        P(FSDP, None, DP),
        P(FSDP, None, DP),
        P(FSDP, None, DP),
        P(FSDP, None, None),
        P(FSDP, DP, None),
    )
    return jax.shard_map(
        local,
        mesh=fine,
        in_specs=placed,
        out_specs=(P(FSDP, None, DP), P(FSDP, None, DP), P(FSDP, None, DP)),
        check_vma=False,
    )
```

```python
import functools

import jax
import jax.numpy as jnp
import numpy as np
from jax import lax
from jax.experimental import pallas as pl
from jax.experimental.pallas import tpu as pltpu
from jax.sharding import Mesh, PartitionSpec as P

FSDP = ("z", "y", "x_lo")
DP = ("x_hi", "core")
SWAP = [(0, 1), (1, 0)]
F32 = jnp.float32
BF16 = jnp.bfloat16
BS = 1024
NB = 64
ROWS = 16
Q = 256
PARTS = 2
PLAIN = ((1,), (0,))
PARAMS = pltpu.CompilerParams(vmem_limit_bytes=16 << 20)


def dot_f32(a, b, dims=PLAIN):
    return lax.dot_general(a, b, (dims, ((), ())), preferred_element_type=F32)


def cost(flops, moved):
    return pl.CostEstimate(flops=flops, bytes_accessed=moved, transcendentals=0)


SWAP_ROWS = np.eye(Q, dtype=np.float32).reshape(ROWS, ROWS, Q).transpose(1, 0, 2).reshape(Q, Q)


def group_at(n, at):
    chip = at[0] if n < 2 else 1 - at[0]
    return 2 * chip + (at[1] if n % 2 == 0 else 1 - at[1])


def group_specs(shape, lead):
    return [
        pl.BlockSpec(shape, lambda i, at, n=n: (0,) * lead + (group_at(n, at),)) for n in range(4)
    ]


def split_kernel(at, *refs):
    for n in range(4):
        refs[4 + n][...] = refs[n][...]


def split(at, grads):
    held = pl.BlockSpec((ROWS, NB, Q), lambda i, at: (0, 0, 0))
    return pl.pallas_call(
        split_kernel,
        grid_spec=pltpu.PrefetchScalarGridSpec(
            num_scalar_prefetch=1,
            grid=(1,),
            in_specs=group_specs((ROWS, NB, Q), 2),
            out_specs=[held] * 4,
        ),
        out_shape=[jax.ShapeDtypeStruct((ROWS, NB, Q), BF16)] * 4,
        compiler_params=PARAMS,
        cost_estimate=cost(0, 4 << 20),
        name="split",
    )(at, grads, grads, grads, grads)


def arrange_kernel(at, *refs):
    for n in range(4):
        refs[4][n] = refs[n][...]


def arrange(at, right):
    return pl.pallas_call(
        arrange_kernel,
        grid_spec=pltpu.PrefetchScalarGridSpec(
            num_scalar_prefetch=1,
            grid=(1,),
            in_specs=group_specs((Q, Q), 1),
            out_specs=pl.BlockSpec((4, Q, Q), lambda i, at: (0, 0, 0)),
        ),
        out_shape=jax.ShapeDtypeStruct((4, Q, Q), BF16),
        compiler_params=PARAMS,
        cost_estimate=cost(0, 1 << 20),
        name="arrange",
    )(at, right, right, right, right)


def whole(kernel, outs, *args, flops=0, name):
    def spec(value):
        return pl.BlockSpec(value.shape, lambda i, rank=len(value.shape): (0,) * rank)

    return pl.pallas_call(
        kernel,
        grid=(1,),
        in_specs=[spec(value) for value in args],
        out_specs=[spec(value) for value in outs],
        out_shape=outs,
        compiler_params=PARAMS,
        cost_estimate=cost(flops, 1 << 10),
        name=name,
    )(*args)


def shape(*dims, kind=BF16):
    return jax.ShapeDtypeStruct(dims, kind)


def pack_kernel(swap_ref, kept, arrived, out):
    swap = swap_ref[...]
    for part in range(NB // ROWS):
        here = pl.ds(part * ROWS, ROWS)
        total = dot_f32(swap, kept[:, here, :].reshape(Q, Q)) + dot_f32(swap, arrived[:, here, :].reshape(Q, Q))
        out[here] = total.astype(out.dtype).reshape(ROWS, ROWS, Q)


def pack(kept, arrived, kind):
    swap = jnp.asarray(SWAP_ROWS, BF16)
    return whole(pack_kernel, [shape(NB, ROWS, Q, kind=kind)], swap, kept, arrived, name="pack")[0]


def add_kernel(here, there, out):
    out[...] = (here[...] + there[...].astype(F32)).astype(BF16)


def add(here, there):
    return whole(add_kernel, [shape(NB, ROWS, Q)], here, there, name="add")[0]


def flip_kernel(values, out):
    out[...] = values[...].T


def flip(values):
    tile = 512
    return pl.pallas_call(
        flip_kernel,
        grid=(BS // tile, BS // tile),
        in_specs=[pl.BlockSpec((tile, tile), lambda i, j: (i, j))],
        out_specs=pl.BlockSpec((tile, tile), lambda i, j: (j, i)),
        out_shape=jax.ShapeDtypeStruct((BS, BS), BF16),
        compiler_params=PARAMS,
        cost_estimate=cost(0, 8 << 20),
        name="flip",
    )(values)


def term_kernel(part, left, grad, right, send, keep):
    size = send.shape[1]
    rotated_left = dot_f32(left[part * size : (part + 1) * size], grad[...]).astype(BF16)
    for chip in range(2):
        send[chip] = dot_f32(rotated_left, right[2 * chip + 1]).astype(BF16)
        keep[chip] = dot_f32(rotated_left, right[2 * chip])


def term(part, left_turned, grad, right):
    size = BS // PARTS
    outs = [shape(2, size, Q), shape(2, size, Q, kind=F32)]
    flops = 16 * size * Q * Q
    kernel = functools.partial(term_kernel, part)
    return whole(kernel, outs, left_turned, grad, right, flops=flops, name="term")


def chip_kernel(kept, arrived, send, keep):
    send[...] = (kept[1] + arrived[1].astype(F32)).astype(BF16)
    keep[...] = kept[0] + arrived[0].astype(F32)


def chip_sum(kept, arrived):
    size = BS // PARTS
    return whole(chip_kernel, [shape(size, Q), shape(size, Q, kind=F32)], kept, arrived, name="chip_sum")


def adam_kernel(part, own, far, m1, m2, *rest):
    first, second, direction = rest[-3:]
    size = own.shape[0]
    rows = slice(part * size, (part + 1) * size)
    rotated = own[...] + far[...].astype(F32)
    new1 = 0.9 * m1[0, rows] + 0.1 * rotated
    new2 = 0.95 * m2[0, rows] + 0.05 * rotated * rotated
    first[0] = new1
    second[0] = new2
    bias_first = 1.0 - 0.9**10
    bias_second = 1.0 - 0.95**10
    direction[...] = (new1 / bias_first / (jnp.sqrt(new2 / bias_second) + 1e-08)).astype(BF16)


def adam(part, own, far, moments, done):
    size = BS // PARTS
    rows = pl.BlockSpec((size, Q), lambda i: (0, 0))
    old = pl.BlockSpec((1, BS, Q), lambda i: (0, 0, 0))
    new = pl.BlockSpec((1, size, Q), lambda i: (0, part, 0))
    return pl.pallas_call(
        functools.partial(adam_kernel, part),
        grid=(1,),
        in_specs=[rows] * 2 + [old] * 2 + [pl.BlockSpec(memory_space=pl.ANY)] * len(done),
        out_specs=[new, new, rows],
        out_shape=[shape(1, BS, Q, kind=F32), shape(1, BS, Q, kind=F32), shape(size, Q)],
        input_output_aliases={4 + n: n for n in range(len(done))},
        compiler_params=PARAMS,
        cost_estimate=cost(1 << 10, 1 << 10),
        name="adam",
    )(own, far, *moments, *done)


def turn_kernel(own, near, far, right, *rest):
    *cross, out = rest
    both = ((1,), (1,))
    size = out.shape[0] // len(cross)
    for n, piece in enumerate(cross):
        rows = slice(n * size, (n + 1) * size)
        total = dot_f32(own[rows], right[0], both) + dot_f32(near[rows], right[1], both)
        total += dot_f32(far[rows], right[2], both) + dot_f32(piece[...], right[3], both)
        out[rows] = total.astype(BF16)


def turn(own, near, far, cross, right):
    return whole(turn_kernel, [shape(BS // PARTS, Q)], own, near, far, right, *cross, name="turn")[0]


def update_kernel(left, turned0, turned1, out):
    size = BS // PARTS
    total = dot_f32(left[:, :size], turned0[...]) + dot_f32(left[:, size:], turned1[...])
    out[...] = total.astype(BF16).reshape(out.shape)


def update(left, *turned):
    return whole(update_kernel, [shape(NB, ROWS, Q)], left, *turned, name="update")[0]


def apply_kernel(swap_ref, pieces, weights, out):
    swap = swap_ref[...]
    for part in range(NB // ROWS):
        here = pl.ds(part * ROWS, ROWS)
        total = dot_f32(swap, pieces[here].reshape(Q, Q))
        out[:, here, :] = weights[:, here, :] - 0.5 * total.reshape(ROWS, ROWS, Q)


def apply(pieces, weights):
    swap = jnp.asarray(SWAP_ROWS, BF16)
    return whole(apply_kernel, [shape(ROWS, NB, Q, kind=F32)], swap, pieces, weights, name="apply")[0]


def exchange(pieces):
    return lax.all_to_all(pieces, FSDP, split_axis=0, concat_axis=0, tiled=True)


def local(grads, weights, moment_first, moment_second, left_basis, right_basis):
    core = lax.axis_index("core").astype(jnp.int32)
    x_hi = lax.axis_index("x_hi").astype(jnp.int32)
    at = jnp.stack([x_hi, core])
    left = left_basis[0]

    own, near, far, cross = split(at, grads[0])
    near = lax.ppermute(near, "core", SWAP)
    far = pack(far, lax.ppermute(cross, "core", SWAP), BF16)
    there = lax.ppermute(far, "x_hi", SWAP)
    far, near = lax.optimization_barrier((far, near))
    here = pack(own, near, F32)
    there, here, left_turned, right = lax.optimization_barrier((there, here, flip(left), arrange(at, right_basis[0])))

    grad_block = exchange(add(here, there)).reshape(BS, Q)

    parts = range(PARTS)
    sent, kept = [], []
    for part in parts:
        send, keep = term(part, left_turned, grad_block, right)
        sent.append(lax.ppermute(send, "core", SWAP))
        kept.append(keep)
    sums = [chip_sum(kept[part], sent[part]) for part in parts]
    arrived = [lax.ppermute(send, "x_hi", SWAP) for send, _ in sums]
    arrived[0], sums[1] = lax.optimization_barrier((arrived[0], sums[1]))
    moments = (moment_first, moment_second)
    *done, own0 = adam(0, sums[0][1], arrived[0], moments, ())
    far0, near0 = lax.ppermute(own0, "x_hi", SWAP), lax.ppermute(own0, "core", SWAP)
    arrived[1], own0 = lax.optimization_barrier((arrived[1], own0))
    *done, own1 = adam(1, sums[1][1], arrived[1], moments, done)
    far1, near1 = lax.ppermute(own1, "x_hi", SWAP), lax.ppermute(own1, "core", SWAP)
    far0, own1 = lax.optimization_barrier((far0, own1))
    quarter = BS // PARTS // 2
    cross0 = [lax.ppermute(far0[n * quarter : (n + 1) * quarter], "core", SWAP) for n in range(2)]
    turned0 = turn(own0, near0, far0, cross0, right)
    far1, turned0 = lax.optimization_barrier((far1, turned0))
    turned1 = turn(own1, near1, far1, [lax.ppermute(far1, "core", SWAP)], right)

    return (apply(exchange(update(left, turned0, turned1)), weights), *done)


def solution(mesh):
    fine = Mesh(mesh.devices.reshape(8, 4, 2, 2, 2), FSDP + DP)
    placed = (
        P(DP, FSDP, None, None),
        P(FSDP, None, DP),
        P(FSDP, None, DP),
        P(FSDP, None, DP),
        P(FSDP, None, None),
        P(FSDP, DP, None),
    )
    return jax.shard_map(
        local,
        mesh=fine,
        in_specs=placed,
        out_specs=(P(FSDP, None, DP), P(FSDP, None, DP), P(FSDP, None, DP)),
        check_vma=False,
    )
```

```python
import functools

import jax
import jax.numpy as jnp
import numpy as np
from jax import lax
from jax.experimental import pallas as pl
from jax.experimental.pallas import tpu as pltpu
from jax.sharding import Mesh, PartitionSpec as P

FSDP = ("z", "y", "x_lo")
DP = ("x_hi", "core")
SWAP = [(0, 1), (1, 0)]
F32 = jnp.float32
BF16 = jnp.bfloat16
BS = 1024
NB = 64
ROWS = 16
Q = 256
PARTS = 2
PLAIN = ((1,), (0,))
PARAMS = pltpu.CompilerParams(vmem_limit_bytes=16 << 20)


def dot_f32(a, b, dims=PLAIN):
    return lax.dot_general(a, b, (dims, ((), ())), preferred_element_type=F32)


def cost(flops, moved):
    return pl.CostEstimate(flops=flops, bytes_accessed=moved, transcendentals=0)


SWAP_ROWS = np.eye(Q, dtype=np.float32).reshape(ROWS, ROWS, Q).transpose(1, 0, 2).reshape(Q, Q)


def group_at(n, at):
    chip = at[0] if n < 2 else 1 - at[0]
    return 2 * chip + (at[1] if n % 2 == 0 else 1 - at[1])


def group_specs(shape, lead):
    return [
        pl.BlockSpec(shape, lambda i, at, n=n: (0,) * lead + (group_at(n, at),)) for n in range(4)
    ]


def split_kernel(at, own, near, far, cross, own_out, near_out, far_out, cross_low, cross_high):
    own_out[...] = own[...]
    near_out[...] = near[...]
    far_out[...] = far[...]
    cross_low[...] = cross[:, : NB // 2]
    cross_high[...] = cross[:, NB // 2 :]


def split(at, grads):
    held = pl.BlockSpec((ROWS, NB, Q), lambda i, at: (0, 0, 0))
    half = pl.BlockSpec((ROWS, NB // 2, Q), lambda i, at: (0, 0, 0))
    return pl.pallas_call(
        split_kernel,
        grid_spec=pltpu.PrefetchScalarGridSpec(
            num_scalar_prefetch=1,
            grid=(1,),
            in_specs=group_specs((ROWS, NB, Q), 2),
            out_specs=[held] * 3 + [half] * 2,
        ),
        out_shape=[shape(ROWS, NB, Q)] * 3 + [shape(ROWS, NB // 2, Q)] * 2,
        compiler_params=PARAMS,
        cost_estimate=cost(0, 4 << 20),
        name="split",
    )(at, grads, grads, grads, grads)


def arrange_kernel(at, *refs):
    for n in range(4):
        refs[4][n] = refs[n][...]


def arrange(at, right):
    return pl.pallas_call(
        arrange_kernel,
        grid_spec=pltpu.PrefetchScalarGridSpec(
            num_scalar_prefetch=1,
            grid=(1,),
            in_specs=group_specs((Q, Q), 1),
            out_specs=pl.BlockSpec((4, Q, Q), lambda i, at: (0, 0, 0)),
        ),
        out_shape=jax.ShapeDtypeStruct((4, Q, Q), BF16),
        compiler_params=PARAMS,
        cost_estimate=cost(0, 1 << 20),
        name="arrange",
    )(at, right, right, right, right)


def whole(kernel, outs, *args, flops=0, name):
    def spec(value):
        return pl.BlockSpec(value.shape, lambda i, rank=len(value.shape): (0,) * rank)

    return pl.pallas_call(
        kernel,
        grid=(1,),
        in_specs=[spec(value) for value in args],
        out_specs=[spec(value) for value in outs],
        out_shape=outs,
        compiler_params=PARAMS,
        cost_estimate=cost(flops, 1 << 10),
        name=name,
    )(*args)


def shape(*dims, kind=BF16):
    return jax.ShapeDtypeStruct(dims, kind)


def pack_kernel(first, swap_ref, kept, arrived, out):
    swap = swap_ref[...]
    for part in range(out.shape[0] // ROWS):
        here = slice(part * ROWS, (part + 1) * ROWS)
        there = slice(first + part * ROWS, first + (part + 1) * ROWS)
        total = dot_f32(swap, kept[:, there, :].reshape(Q, Q)) + dot_f32(swap, arrived[:, here, :].reshape(Q, Q))
        out[here] = total.astype(out.dtype).reshape(ROWS, ROWS, Q)


def pack(first, kept, arrived, kind):
    swap = jnp.asarray(SWAP_ROWS, BF16)
    outs = [shape(arrived.shape[1], ROWS, Q, kind=kind)]
    return whole(functools.partial(pack_kernel, first), outs, swap, kept, arrived, name="pack")[0]


def add_kernel(here, low, high, out):
    half = NB // 2
    out[:half] = (here[:half] + low[...].astype(F32)).astype(BF16)
    out[half:] = (here[half:] + high[...].astype(F32)).astype(BF16)


def add(here, low, high):
    return whole(add_kernel, [shape(NB, ROWS, Q)], here, low, high, name="add")[0]


def flip_kernel(values, out):
    out[...] = values[...].T


def flip(values):
    tile = 512
    return pl.pallas_call(
        flip_kernel,
        grid=(BS // tile, BS // tile),
        in_specs=[pl.BlockSpec((tile, tile), lambda i, j: (i, j))],
        out_specs=pl.BlockSpec((tile, tile), lambda i, j: (j, i)),
        out_shape=jax.ShapeDtypeStruct((BS, BS), BF16),
        compiler_params=PARAMS,
        cost_estimate=cost(0, 8 << 20),
        name="flip",
    )(values)


def term_kernel(part, left, grad, right, send, keep):
    size = send.shape[1]
    rotated_left = dot_f32(left[part * size : (part + 1) * size], grad[...]).astype(BF16)
    for chip in range(2):
        send[chip] = dot_f32(rotated_left, right[2 * chip + 1]).astype(BF16)
        keep[chip] = dot_f32(rotated_left, right[2 * chip])


def term(part, left_turned, grad, right):
    size = BS // PARTS
    outs = [shape(2, size, Q), shape(2, size, Q, kind=F32)]
    flops = 16 * size * Q * Q
    kernel = functools.partial(term_kernel, part)
    return whole(kernel, outs, left_turned, grad, right, flops=flops, name="term")


def chip_kernel(kept, arrived, send, keep):
    send[...] = (kept[1] + arrived[1].astype(F32)).astype(BF16)
    keep[...] = kept[0] + arrived[0].astype(F32)


def chip_sum(kept, arrived):
    size = BS // PARTS
    return whole(chip_kernel, [shape(size, Q), shape(size, Q, kind=F32)], kept, arrived, name="chip_sum")


def moments_of(rotated, m1, m2):
    return 0.9 * m1 + 0.1 * rotated, 0.95 * m2 + 0.05 * rotated * rotated


def adam_kernel(part, own, far, m1, m2, rotated, direction):
    size = own.shape[0]
    rows = slice(part * size, (part + 1) * size)
    rotated[...] = own[...] + far[...].astype(F32)
    new1, new2 = moments_of(rotated[...], m1[0, rows], m2[0, rows])
    bias_first = 1.0 - 0.9**10
    bias_second = 1.0 - 0.95**10
    direction[...] = (new1 / bias_first / (jnp.sqrt(new2 / bias_second) + 1e-08)).astype(BF16)


def adam(part, own, far, moments):
    size = BS // PARTS
    kernel = functools.partial(adam_kernel, part)
    return whole(kernel, [shape(size, Q, kind=F32), shape(size, Q)], own, far, *moments, name="adam")


def moments_kernel(rotated0, rotated1, m1, m2, first, second):
    size = BS // PARTS
    for part, rotated in enumerate((rotated0, rotated1)):
        rows = slice(part * size, (part + 1) * size)
        first[0, rows], second[0, rows] = moments_of(rotated[...], m1[0, rows], m2[0, rows])


def new_moments(rotated, moments):
    outs = [shape(1, BS, Q, kind=F32)] * 2
    return whole(moments_kernel, outs, *rotated, *moments, name="moments")


def turn_kernel(own, near, far, right, *rest):
    *cross, out = rest
    both = ((1,), (1,))
    size = out.shape[0] // len(cross)
    for n, piece in enumerate(cross):
        rows = slice(n * size, (n + 1) * size)
        total = dot_f32(own[rows], right[0], both) + dot_f32(near[rows], right[1], both)
        total += dot_f32(far[rows], right[2], both) + dot_f32(piece[...], right[3], both)
        out[rows] = total.astype(BF16)


def turn(own, near, far, cross, right):
    return whole(turn_kernel, [shape(BS // PARTS, Q)], own, near, far, right, *cross, name="turn")[0]


def update_kernel(left, turned0, turned1, out):
    size = BS // PARTS
    total = dot_f32(left[:, :size], turned0[...]) + dot_f32(left[:, size:], turned1[...])
    out[...] = total.astype(BF16).reshape(out.shape)


def update(left, *turned):
    return whole(update_kernel, [shape(NB, ROWS, Q)], left, *turned, name="update")[0]


def apply_kernel(swap_ref, pieces, weights, out):
    swap = swap_ref[...]
    for part in range(NB // ROWS):
        here = pl.ds(part * ROWS, ROWS)
        total = dot_f32(swap, pieces[here].reshape(Q, Q))
        out[:, here, :] = weights[:, here, :] - 0.5 * total.reshape(ROWS, ROWS, Q)


def apply(pieces, weights):
    swap = jnp.asarray(SWAP_ROWS, BF16)
    return whole(apply_kernel, [shape(ROWS, NB, Q, kind=F32)], swap, pieces, weights, name="apply")[0]


def exchange(pieces):
    return lax.all_to_all(pieces, FSDP, split_axis=0, concat_axis=0, tiled=True)


def local(grads, weights, moment_first, moment_second, left_basis, right_basis):
    core = lax.axis_index("core").astype(jnp.int32)
    x_hi = lax.axis_index("x_hi").astype(jnp.int32)
    at = jnp.stack([x_hi, core])
    left = left_basis[0]

    own, near, far, low, high = split(at, grads[0])
    low, high, near = (lax.ppermute(value, "core", SWAP) for value in (low, high, near))
    low = pack(0, far, low, BF16)
    low_there = lax.ppermute(low, "x_hi", SWAP)
    low, high = lax.optimization_barrier((low, high))
    high = pack(NB // 2, far, high, BF16)
    high_there = lax.ppermute(high, "x_hi", SWAP)
    high, near = lax.optimization_barrier((high, near))
    here = pack(0, own, near, F32)
    low_there, high_there, here, left_turned, right = lax.optimization_barrier(
        (low_there, high_there, here, flip(left), arrange(at, right_basis[0]))
    )

    grad_block = exchange(add(here, low_there, high_there)).reshape(BS, Q)

    parts = range(PARTS)
    sent, kept = [], []
    for part in parts:
        send, keep = term(part, left_turned, grad_block, right)
        sent.append(lax.ppermute(send, "core", SWAP))
        kept.append(keep)
    sums = [chip_sum(kept[part], sent[part]) for part in parts]
    arrived = [lax.ppermute(send, "x_hi", SWAP) for send, _ in sums]
    arrived[0], sums[1] = lax.optimization_barrier((arrived[0], sums[1]))
    moments = (moment_first, moment_second)
    rotated0, own0 = adam(0, sums[0][1], arrived[0], moments)
    far0, near0 = lax.ppermute(own0, "x_hi", SWAP), lax.ppermute(own0, "core", SWAP)
    arrived[1], own0 = lax.optimization_barrier((arrived[1], own0))
    rotated1, own1 = adam(1, sums[1][1], arrived[1], moments)
    far1, near1 = lax.ppermute(own1, "x_hi", SWAP), lax.ppermute(own1, "core", SWAP)
    first_new, second_new = new_moments((rotated0, rotated1), moments)
    far0, own1, first_new, second_new = lax.optimization_barrier((far0, own1, first_new, second_new))
    quarter = BS // PARTS // 2
    cross0 = [lax.ppermute(far0[n * quarter : (n + 1) * quarter], "core", SWAP) for n in range(2)]
    turned0 = turn(own0, near0, far0, cross0, right)
    far1, turned0 = lax.optimization_barrier((far1, turned0))
    turned1 = turn(own1, near1, far1, [lax.ppermute(far1, "core", SWAP)], right)

    return (apply(exchange(update(left, turned0, turned1)), weights), first_new, second_new)


def solution(mesh):
    fine = Mesh(mesh.devices.reshape(8, 4, 2, 2, 2), FSDP + DP)
    placed = (
        P(DP, FSDP, None, None),
        P(FSDP, None, DP),
        P(FSDP, None, DP),
        P(FSDP, None, DP),
        P(FSDP, None, None),
        P(FSDP, DP, None),
    )
    return jax.shard_map(
        local,
        mesh=fine,
        in_specs=placed,
        out_specs=(P(FSDP, None, DP), P(FSDP, None, DP), P(FSDP, None, DP)),
        check_vma=False,
    )
```

```python
import functools

import jax
import jax.numpy as jnp
import numpy as np
from jax import lax
from jax.experimental import pallas as pl
from jax.experimental.pallas import tpu as pltpu
from jax.sharding import Mesh, PartitionSpec as P

FSDP = ("z", "y", "x_lo")
DP = ("x_hi", "core")
SWAP = [(0, 1), (1, 0)]
F32 = jnp.float32
BF16 = jnp.bfloat16
BS = 1024
NB = 64
ROWS = 16
Q = 256
PARTS = 2
PLAIN = ((1,), (0,))
PARAMS = pltpu.CompilerParams(vmem_limit_bytes=16 << 20)


def dot_f32(a, b, dims=PLAIN):
    return lax.dot_general(a, b, (dims, ((), ())), preferred_element_type=F32)


def cost(flops, moved):
    return pl.CostEstimate(flops=flops, bytes_accessed=moved, transcendentals=0)


SWAP_ROWS = np.eye(Q, dtype=np.float32).reshape(ROWS, ROWS, Q).transpose(1, 0, 2).reshape(Q, Q)


def group_at(n, at):
    chip = at[0] if n < 2 else 1 - at[0]
    return 2 * chip + (at[1] if n % 2 == 0 else 1 - at[1])


def group_specs(shape, lead):
    return [
        pl.BlockSpec(shape, lambda i, at, n=n: (0,) * lead + (group_at(n, at),)) for n in range(4)
    ]


def split_kernel(at, *refs):
    for n in range(4):
        refs[4 + n][...] = refs[n][...]


def split(at, grads):
    held = pl.BlockSpec((ROWS, NB, Q), lambda i, at: (0, 0, 0))
    return pl.pallas_call(
        split_kernel,
        grid_spec=pltpu.PrefetchScalarGridSpec(
            num_scalar_prefetch=1,
            grid=(1,),
            in_specs=group_specs((ROWS, NB, Q), 2),
            out_specs=[held] * 4,
        ),
        out_shape=[jax.ShapeDtypeStruct((ROWS, NB, Q), BF16)] * 4,
        compiler_params=PARAMS,
        cost_estimate=cost(0, 4 << 20),
        name="split",
    )(at, grads, grads, grads, grads)


def arrange_kernel(at, *refs):
    for n in range(4):
        refs[4][n] = refs[n][...]


def arrange(at, right):
    return pl.pallas_call(
        arrange_kernel,
        grid_spec=pltpu.PrefetchScalarGridSpec(
            num_scalar_prefetch=1,
            grid=(1,),
            in_specs=group_specs((Q, Q), 1),
            out_specs=pl.BlockSpec((4, Q, Q), lambda i, at: (0, 0, 0)),
        ),
        out_shape=jax.ShapeDtypeStruct((4, Q, Q), BF16),
        compiler_params=PARAMS,
        cost_estimate=cost(0, 1 << 20),
        name="arrange",
    )(at, right, right, right, right)


def whole(kernel, outs, *args, flops=0, name):
    def spec(value):
        return pl.BlockSpec(value.shape, lambda i, rank=len(value.shape): (0,) * rank)

    return pl.pallas_call(
        kernel,
        grid=(1,),
        in_specs=[spec(value) for value in args],
        out_specs=[spec(value) for value in outs],
        out_shape=outs,
        compiler_params=PARAMS,
        cost_estimate=cost(flops, 1 << 10),
        name=name,
    )(*args)


def shape(*dims, kind=BF16):
    return jax.ShapeDtypeStruct(dims, kind)


def pack_kernel(swap_ref, kept, arrived, out):
    swap = swap_ref[...]
    for part in range(NB // ROWS):
        here = pl.ds(part * ROWS, ROWS)
        total = dot_f32(swap, kept[:, here, :].reshape(Q, Q)) + dot_f32(swap, arrived[:, here, :].reshape(Q, Q))
        out[here] = total.astype(out.dtype).reshape(ROWS, ROWS, Q)


def pack(kept, arrived, kind):
    swap = jnp.asarray(SWAP_ROWS, BF16)
    return whole(pack_kernel, [shape(NB, ROWS, Q, kind=kind)], swap, kept, arrived, name="pack")[0]


def add_kernel(here, there, out):
    out[...] = (here[...] + there[...].astype(F32)).astype(BF16)


def add(here, there):
    return whole(add_kernel, [shape(NB, ROWS, Q)], here, there, name="add")[0]


def flip_kernel(values, out):
    out[...] = values[...].T


def flip(values):
    tile = 512
    return pl.pallas_call(
        flip_kernel,
        grid=(BS // tile, BS // tile),
        in_specs=[pl.BlockSpec((tile, tile), lambda i, j: (i, j))],
        out_specs=pl.BlockSpec((tile, tile), lambda i, j: (j, i)),
        out_shape=jax.ShapeDtypeStruct((BS, BS), BF16),
        compiler_params=PARAMS,
        cost_estimate=cost(0, 8 << 20),
        name="flip",
    )(values)


def term_kernel(part, left, grad, right, send, keep):
    size = send.shape[1]
    rotated_left = dot_f32(left[part * size : (part + 1) * size], grad[...]).astype(BF16)
    for chip in range(2):
        send[chip] = dot_f32(rotated_left, right[2 * chip + 1]).astype(BF16)
        keep[chip] = dot_f32(rotated_left, right[2 * chip])


def term(part, left_turned, grad, right):
    size = BS // PARTS
    outs = [shape(2, size, Q), shape(2, size, Q, kind=F32)]
    flops = 16 * size * Q * Q
    kernel = functools.partial(term_kernel, part)
    return whole(kernel, outs, left_turned, grad, right, flops=flops, name="term")


def chip_kernel(kept, arrived, send, keep):
    send[...] = (kept[1] + arrived[1].astype(F32)).astype(BF16)
    keep[...] = kept[0] + arrived[0].astype(F32)


def chip_sum(kept, arrived):
    size = BS // PARTS
    return whole(chip_kernel, [shape(size, Q), shape(size, Q, kind=F32)], kept, arrived, name="chip_sum")


def moments_of(rotated, m1, m2):
    return 0.9 * m1 + 0.1 * rotated, 0.95 * m2 + 0.05 * rotated * rotated


def adam_kernel(part, own, far, m1, m2, rotated, direction):
    size = own.shape[0]
    rows = slice(part * size, (part + 1) * size)
    rotated[...] = own[...] + far[...].astype(F32)
    new1, new2 = moments_of(rotated[...], m1[0, rows], m2[0, rows])
    bias_first = 1.0 - 0.9**10
    bias_second = 1.0 - 0.95**10
    direction[...] = (new1 / bias_first / (jnp.sqrt(new2 / bias_second) + 1e-08)).astype(BF16)


def adam(part, own, far, moments):
    size = BS // PARTS
    kernel = functools.partial(adam_kernel, part)
    return whole(kernel, [shape(size, Q, kind=F32), shape(size, Q)], own, far, *moments, name="adam")


def moments_kernel(rotated0, rotated1, m1, m2, first, second):
    size = BS // PARTS
    for part, rotated in enumerate((rotated0, rotated1)):
        rows = slice(part * size, (part + 1) * size)
        first[0, rows], second[0, rows] = moments_of(rotated[...], m1[0, rows], m2[0, rows])


def new_moments(rotated, moments):
    outs = [shape(1, BS, Q, kind=F32)] * 2
    return whole(moments_kernel, outs, *rotated, *moments, name="moments")


def turn_kernel(own, near, far, right, *rest):
    *cross, out = rest
    both = ((1,), (1,))
    size = out.shape[0] // len(cross)
    for n, piece in enumerate(cross):
        rows = slice(n * size, (n + 1) * size)
        total = dot_f32(own[rows], right[0], both) + dot_f32(near[rows], right[1], both)
        total += dot_f32(far[rows], right[2], both) + dot_f32(piece[...], right[3], both)
        out[rows] = total.astype(BF16)


def turn(own, near, far, cross, right):
    return whole(turn_kernel, [shape(BS // PARTS, Q)], own, near, far, right, *cross, name="turn")[0]


def update_kernel(left, turned0, turned1, out):
    size = BS // PARTS
    total = dot_f32(left[:, :size], turned0[...]) + dot_f32(left[:, size:], turned1[...])
    out[...] = total.astype(BF16).reshape(out.shape)


def update(left, *turned):
    return whole(update_kernel, [shape(NB, ROWS, Q)], left, *turned, name="update")[0]


def apply_kernel(swap_ref, pieces, weights, out):
    swap = swap_ref[...]
    for part in range(NB // ROWS):
        here = pl.ds(part * ROWS, ROWS)
        total = dot_f32(swap, pieces[here].reshape(Q, Q))
        out[:, here, :] = weights[:, here, :] - 0.5 * total.reshape(ROWS, ROWS, Q)


def apply(pieces, weights):
    swap = jnp.asarray(SWAP_ROWS, BF16)
    return whole(apply_kernel, [shape(ROWS, NB, Q, kind=F32)], swap, pieces, weights, name="apply")[0]


def exchange(pieces):
    return lax.all_to_all(pieces, FSDP, split_axis=0, concat_axis=0, tiled=True)


def local(grads, weights, moment_first, moment_second, left_basis, right_basis):
    core = lax.axis_index("core").astype(jnp.int32)
    x_hi = lax.axis_index("x_hi").astype(jnp.int32)
    at = jnp.stack([x_hi, core])
    left = left_basis[0]

    own, near, far, cross = split(at, grads[0])
    near = lax.ppermute(near, "core", SWAP)
    far = pack(far, lax.ppermute(cross, "core", SWAP), BF16)
    there = lax.ppermute(far, "x_hi", SWAP)
    far, near = lax.optimization_barrier((far, near))
    here = pack(own, near, F32)
    there, here, left_turned, right = lax.optimization_barrier((there, here, flip(left), arrange(at, right_basis[0])))

    grad_block = exchange(add(here, there)).reshape(BS, Q)

    parts = range(PARTS)
    sent, kept = [], []
    for part in parts:
        send, keep = term(part, left_turned, grad_block, right)
        sent.append(lax.ppermute(send, "core", SWAP))
        kept.append(keep)
    sums = [chip_sum(kept[part], sent[part]) for part in parts]
    arrived = [lax.ppermute(send, "x_hi", SWAP) for send, _ in sums]
    arrived[0], sums[1] = lax.optimization_barrier((arrived[0], sums[1]))
    moments = (moment_first, moment_second)
    rotated0, own0 = adam(0, sums[0][1], arrived[0], moments)
    far0, near0 = lax.ppermute(own0, "x_hi", SWAP), lax.ppermute(own0, "core", SWAP)
    arrived[1], own0 = lax.optimization_barrier((arrived[1], own0))
    rotated1, own1 = adam(1, sums[1][1], arrived[1], moments)
    far1, near1 = lax.ppermute(own1, "x_hi", SWAP), lax.ppermute(own1, "core", SWAP)
    first_new, second_new = new_moments((rotated0, rotated1), moments)
    far0, own1, first_new, second_new = lax.optimization_barrier((far0, own1, first_new, second_new))
    quarter = BS // PARTS // 2
    cross0 = [lax.ppermute(far0[n * quarter : (n + 1) * quarter], "core", SWAP) for n in range(2)]
    turned0 = turn(own0, near0, far0, cross0, right)
    far1, turned0 = lax.optimization_barrier((far1, turned0))
    turned1 = turn(own1, near1, far1, [lax.ppermute(far1, "core", SWAP)], right)

    return (apply(exchange(update(left, turned0, turned1)), weights), first_new, second_new)


def solution(mesh):
    fine = Mesh(mesh.devices.reshape(8, 4, 2, 2, 2), FSDP + DP)
    placed = (
        P(DP, FSDP, None, None),
        P(FSDP, None, DP),
        P(FSDP, None, DP),
        P(FSDP, None, DP),
        P(FSDP, None, None),
        P(FSDP, DP, None),
    )
    return jax.shard_map(
        local,
        mesh=fine,
        in_specs=placed,
        out_specs=(P(FSDP, None, DP), P(FSDP, None, DP), P(FSDP, None, DP)),
        check_vma=False,
    )
```
